512 devices in a mesh: rep: 4 (over y), fsdp: 128 (over z, x, core).
Axes of the slice: x: 4, y: 4, z: 16, core: 2. Of those that a mesh axis runs over, the one named last changes fastest.
Arguments:
- gradient: bfloat16 [4, 64, 512, 512], P('rep', None, 'fsdp'), may hold values from -1.6953125 to 1.6953125
- left_stats: float32 [128, 512, 512], P('fsdp'), as said below
- right_stats: float32 [128, 512, 512], P('fsdp'), as said below
- block_lists: int32 [128, 1], replicated, may hold values from -1 to 63, as said below
- block_counts: int32 [128], replicated, may hold values from 0 to 1, as said below
Outputs:
- direction: bfloat16 [64, 512, 512], P(None, 'fsdp')
- left_new: float32 [128, 512, 512], P('fsdp')
- right_new: float32 [128, 512, 512], P('fsdp')
The draws below stay inside these ranges and needn't reach their ends.
Inputs may be any that keep to these rules, and one draw needn't show every extreme that they name: `block_lists`: entries k < block_counts[w] of row w name the blocks that worker w preconditions; over all workers each of the 64 blocks is named exactly once; all other entries are -1. block_counts[w] is the number of blocks of worker w; some worker holds exactly 1. `left_stats`: each slot's matrix is symmetric positive definite. `right_stats`: each slot's matrix is symmetric positive definite.
All inputs are finite; a program needn't handle non-finite values. Where the reference program divides by a largest or mean magnitude, that divisor is 1e-20 or more.
Results may differ from the reference program's by a relative error of at most 0.015.
Values may be sent and summed in bfloat16 or wider, within the bound.
A program may use at most 64 MiB of HBM per device.

```python
import math
import jax
import jax.numpy as jnp
from jax import lax

BLOCK = 512
ITERS = 2
NBLK = 64
SLOTS = 1
N_REP = 4
N_FSDP = 128


def assignment(key):
    first_key, second_key, third_key = jax.random.split(key, 3)
    slot_total = N_FSDP * SLOTS
    full_worker = jax.random.randint(first_key, (), 0, N_FSDP)
    slot_owner = jnp.arange(slot_total) // SLOTS
    shuffled = jax.random.permutation(second_key, slot_total)
    priority = jnp.where(slot_owner == full_worker, -1, shuffled)
    ranking = jnp.argsort(jnp.argsort(priority, stable=True), stable=True)
    taken_slot = (ranking < NBLK).reshape(N_FSDP, SLOTS)
    counts = jnp.sum(taken_slot.astype(jnp.int32), axis=1)
    offsets = jnp.cumsum(counts) - counts
    blocks_order = jax.random.permutation(third_key, NBLK)
    position = jnp.arange(SLOTS)
    flat_index = jnp.clip(offsets[:, None] + position[None, :], 0, NBLK - 1)
    block_table = jnp.where(position[None, :] < counts[:, None], blocks_order[flat_index], -1)
    return (block_table.astype(jnp.int32), counts.astype(jnp.int32))


def make_stats(key, spread):
    scale_key, diag_key, off_key = jax.random.split(key, 3)
    slot_total = N_FSDP * SLOTS
    row_scale = jnp.exp(jax.random.uniform(scale_key, (slot_total, BLOCK), jnp.float32, 0.0, spread))
    diagonal = 1.5 + 1.5 * jax.random.uniform(diag_key, (slot_total, BLOCK), jnp.float32)
    raw_part = jax.random.uniform(off_key, (slot_total, BLOCK, BLOCK), jnp.float32, -1.0, 1.0) * (1.4 / BLOCK)
    symmetric = 0.5 * (raw_part + jnp.swapaxes(raw_part, 1, 2))
    positions = jnp.arange(BLOCK)
    on_diag = (positions[:, None] == positions[None, :]).astype(jnp.float32)
    core_mat = symmetric * (1.0 - on_diag) + diagonal[:, :, None] * on_diag
    return 8.0 * row_scale[:, :, None] * row_scale[:, None, :] * core_mat


def draw_block_lists(key, part):
    block_table, counts = assignment(key)
    return block_table


def draw_block_counts(key, part):
    block_table, counts = assignment(key)
    return counts


def draw_left_stats(key, part):
    key = jax.random.fold_in(key, 5)
    spread = 0.5 * math.log(10.0)
    return make_stats(key, spread)


def draw_right_stats(key, part):
    key = jax.random.fold_in(key, 9)
    spread = 0.5 * math.log(10.0)
    return make_stats(key, spread)


def block_levels(stream_key, dims, shards, low, largest):
    gain = 1.0
    for dim, shards_of in shards:
        steps = jax.random.uniform(jax.random.fold_in(jax.random.fold_in(stream_key, 6), dim), (shards_of,), jnp.float32, low / len(shards), largest / len(shards))
        gain = gain * jnp.repeat(jnp.exp(steps), dims[dim] // shards_of).reshape((-1,) + (1,) * (len(dims) - 1 - dim))
    return gain


def noise(own_key, dims, width, bound, cuts=(), kind=jnp.bfloat16):
    level = block_levels(own_key, dims, cuts, -0.22, 0.18) if cuts else 1.0
    entries = jax.random.normal(own_key, dims, jnp.float32) * width * level
    return jnp.minimum(jnp.maximum(entries, -bound), bound).astype(kind)


def setup_inputs(seed: int = 0) -> dict:
    arg_keys = jax.random.split(jax.random.key(seed), 6)
    gradient = noise(arg_keys[0], (N_REP, NBLK, BLOCK, BLOCK), 0.28, 1.6953125, ((0, 4), (2, 128)))
    left_stats = draw_left_stats(jax.random.fold_in(arg_keys[5], 71), 0)
    right_stats = draw_right_stats(jax.random.fold_in(arg_keys[5], 71), 0)
    block_lists = draw_block_lists(jax.random.fold_in(arg_keys[5], 71), 0)
    block_counts = draw_block_counts(jax.random.fold_in(arg_keys[5], 71), 0)
    return dict(gradient=gradient, left_stats=left_stats, right_stats=right_stats, block_lists=block_lists, block_counts=block_counts)


decay_rate = 0.95

def hidot(left_mat, right_mat):
    return jnp.dot(left_mat, right_mat, precision=lax.Precision.HIGHEST, preferred_element_type=jnp.float32)

def inverse_root(matrix):
    dimension = matrix.shape[0]
    identity_mat = jnp.eye(dimension, dtype=jnp.float32)
    row_bound = jnp.max(lax.optimization_barrier(jnp.sum(jnp.abs(matrix), axis=1)))
    factor = 2.5 / row_bound
    current = factor * matrix
    root_est = identity_mat
    for sweep in range(ITERS):
        step_mat = (5.0 * identity_mat - current) * 0.25
        if sweep == 0:
            root_est = jnp.sqrt(jnp.sqrt(factor)) * step_mat
        else:
            root_est = hidot(root_est, step_mat)
        if sweep + 1 < ITERS:
            square = hidot(step_mat, step_mat)
            fourth = hidot(square, square)
            current = hidot(fourth, current)
    return root_est

def precondition(grad_block, left_stat, right_stat):
    gram_left = jnp.dot(grad_block, grad_block.T, preferred_element_type=jnp.float32)
    gram_right = jnp.dot(grad_block.T, grad_block, preferred_element_type=jnp.float32)
    left_next = decay_rate * left_stat + (1.0 - decay_rate) * gram_left
    right_next = decay_rate * right_stat + (1.0 - decay_rate) * gram_right
    left_root = inverse_root(left_next).astype(jnp.bfloat16)
    right_root = inverse_root(right_next).astype(jnp.bfloat16)
    half_step = jnp.dot(left_root, grad_block, preferred_element_type=jnp.float32).astype(jnp.bfloat16)
    shaped = jnp.dot(half_step, right_root, preferred_element_type=jnp.float32)
    grad_wide = grad_block.astype(jnp.float32)
    grad_norm = jnp.sqrt(jnp.sum(grad_wide * grad_wide))
    shaped_norm = jnp.sqrt(jnp.sum(shaped * shaped) + 1e-06)
    grafted = (shaped * (grad_norm / shaped_norm)).astype(jnp.bfloat16)
    return (grafted, left_next, right_next)

def skip_slot(grad_block, left_stat, right_stat):
    return (jnp.zeros_like(grad_block), left_stat, right_stat)

def reference(gradient, left_stats, right_stats, block_lists, block_counts):
    summed = lax.optimization_barrier(jnp.sum(gradient.astype(jnp.float32), axis=0)).astype(jnp.bfloat16)
    block_ids = jnp.clip(block_lists, 0, NBLK - 1).astype(jnp.int32).reshape(-1)
    live_slots = (jnp.arange(SLOTS, dtype=jnp.int32)[None, :] < block_counts[:, None]).reshape(-1)

    def one_slot(slot_items):
        block_id, usable, left_stat, right_stat = slot_items
        grad_block = lax.dynamic_index_in_dim(summed, block_id, 0, keepdims=False)
        return lax.cond(usable, precondition, skip_slot, grad_block, left_stat, right_stat)
    grafted, left_new, right_new = lax.map(one_slot, (block_ids, live_slots, left_stats, right_stats))
    targets = jnp.where(live_slots, block_ids, NBLK).astype(jnp.int32)
    direction = jnp.zeros((NBLK, BLOCK, BLOCK), jnp.bfloat16).at[targets].set(grafted, mode='drop')
    return (direction, left_new, right_new)
```

```python
import functools

import jax
import jax.numpy as jnp
from jax import lax
from jax.experimental import pallas as pl
from jax.experimental.pallas import tpu as pltpu
from jax.sharding import PartitionSpec as P

DECAY = 0.95
LANES = 8
MESH = pl.DeviceIdType.MESH


def near_first(count):
    order = []
    for step in range(1, count // 2 + 1):
        order.append(step)
        if count - step != step:
            order.append(count - step)
    return order


def greet(reps, layers):
    rep, place = lax.axis_index("rep"), lax.axis_index("fsdp")
    layer, lane = place // LANES, place % LANES
    barrier = pltpu.get_barrier_semaphore()
    for step in range(1, layers):
        peer = ((layer + step) % layers) * LANES + lane
        pl.semaphore_signal(barrier, inc=1, device_id=(rep, peer), device_id_type=MESH)
    for turn in range(reps):
        for hop in range(LANES):
            if turn or hop:
                peer = layer * LANES + (lane + hop) % LANES
                pl.semaphore_signal(
                    barrier, inc=1, device_id=((rep + turn) % reps, peer), device_id_type=MESH
                )
    pl.semaphore_wait(barrier, layers - 1 + reps * LANES - 1)


def exchange(reps, layers, send, mid, out, a_send, a_recv, b_send, b_recv, own):
    rep, place = lax.axis_index("rep"), lax.axis_index("fsdp")
    layer, lane = place // LANES, place % LANES
    first = []
    for step in near_first(layers)[::-1]:
        there = (layer + step) % layers
        copy = pltpu.make_async_remote_copy(
            src_ref=send.at[there],
            dst_ref=mid.at[:, layer],
            send_sem=a_send.at[step],
            recv_sem=a_recv.at[step],
            device_id=(rep, there * LANES + lane),
            device_id_type=MESH,
        )
        copy.start()
        first.append(copy)
    keep = pltpu.make_async_copy(send.at[layer], mid.at[:, layer], own.at[0])
    keep.start()
    keep.wait()
    for copy in first:
        copy.wait_recv()
    second = []
    for turn in (2, 1, 3, 0) if reps == 4 else range(reps):
        for hop in range(LANES):
            if turn or hop:
                target = (lane + hop) % LANES
                copy = pltpu.make_async_remote_copy(
                    src_ref=mid.at[target],
                    dst_ref=out.at[rep, :, lane],
                    send_sem=b_send.at[turn, hop],
                    recv_sem=b_recv.at[turn, hop],
                    device_id=((rep + turn) % reps, layer * LANES + target),
                    device_id_type=MESH,
                )
                copy.start()
                second.append(copy)
    stay = pltpu.make_async_copy(mid.at[lane], out.at[rep, :, lane], own.at[1])
    stay.start()
    stay.wait()
    for copy in second:
        copy.wait_recv()
    for copy in first + second:
        copy.wait_send()


def exchange_scratch(reps, layers, rows, width):
    return [
        pltpu.VMEM((LANES, layers, rows, width), jnp.bfloat16),
        pltpu.SemaphoreType.DMA((layers,)),
        pltpu.SemaphoreType.DMA((layers,)),
        pltpu.SemaphoreType.DMA((reps, LANES)),
        pltpu.SemaphoreType.DMA((reps, LANES)),
        pltpu.SemaphoreType.DMA((2,)),
    ]


def gather_kernel(
    reps, layers, grad, ids, out, parts, total, send, r_send, r_recv, r_own,
    mid, a_send, a_recv, b_send, b_recv, own,
):
    rep, place = lax.axis_index("rep"), lax.axis_index("fsdp")
    width = total.shape[-1]
    greet(reps, layers)
    copies = []
    for turn in range(1, reps):
        there = (rep + turn) % reps
        copy = pltpu.make_async_remote_copy(
            src_ref=grad.at[0, :, :, pl.ds(pl.multiple_of(there * width, width), width)],
            dst_ref=parts.at[turn],
            send_sem=r_send.at[turn],
            recv_sem=r_recv.at[turn],
            device_id=(there, place),
            device_id_type=MESH,
        )
        copy.start()
        copies.append(copy)
    mine = pltpu.make_async_copy(
        grad.at[0, :, :, pl.ds(pl.multiple_of(rep * width, width), width)], parts.at[0], r_own
    )
    mine.start()
    mine.wait()
    for copy in copies:
        copy.wait_recv()
    acc = parts[0].astype(jnp.float32)
    for turn in range(1, reps):
        acc = acc + parts[turn].astype(jnp.float32)
    total[...] = acc.astype(jnp.bfloat16)

    @pl.loop(0, layers)
    def _(layer):
        for lane in range(LANES):
            send[layer, lane] = total[ids[layer * LANES + lane]]

    exchange(reps, layers, send, mid, out, a_send, a_recv, b_send, b_recv, own)
    for copy in copies:
        copy.wait_send()


def return_kernel(reps, layers, piece, out, mid, a_send, a_recv, b_send, b_recv, own):
    greet(reps, layers)
    exchange(reps, layers, piece, mid, out, a_send, a_recv, b_send, b_recv, own)


def mm(a, b, dims=((1,), (0,))):
    return lax.dot_general(a, b, (dims, ((), ())), preferred_element_type=jnp.float32)


def root(stat):
    size = stat.shape[0]
    bound = jnp.max(jnp.sum(jnp.abs(stat), axis=0, keepdims=True))
    factor = 2.5 / bound
    row = lax.broadcasted_iota(jnp.int32, (size, size), 0)
    col = lax.broadcasted_iota(jnp.int32, (size, size), 1)
    step = jnp.where(row == col, 1.25, 0.0) - (0.25 * factor) * stat
    low = step.astype(jnp.bfloat16)
    square = mm(low, low)
    low2 = square.astype(jnp.bfloat16)
    fourth = mm(low2, low2).astype(jnp.bfloat16)
    inner = (5.0 * step - 4.0 * square).astype(jnp.bfloat16)
    gain = 0.25 * jnp.sqrt(jnp.sqrt(factor))
    return (gain * (5.0 * step - mm(fourth, inner))).astype(jnp.bfloat16)


def block_kernel(
    reps, blocks, left, right, live, left_out, right_out, piece, grad, left_new, right_new,
    shaped, sems,
):
    width = piece.shape[1]
    rep = lax.axis_index("rep")
    for part in range(reps):
        grad[:, part * width : (part + 1) * width] = blocks[part]
    g = grad[...]
    used = live[0] > 0
    gram_left = mm(g, g, ((1,), (1,)))
    left_new[...] = jnp.where(used, DECAY * left[0] + (1.0 - DECAY) * gram_left, left[0])
    put_left = pltpu.make_async_copy(left_new, left_out.at[0], sems.at[0])
    put_left.start()
    gram_right = mm(g, g, ((0,), (0,)))
    right_new[...] = jnp.where(used, DECAY * right[0] + (1.0 - DECAY) * gram_right, right[0])
    put_right = pltpu.make_async_copy(right_new, right_out.at[0], sems.at[1])
    put_right.start()
    left_root = root(left_new[...])
    right_root = root(right_new[...])
    half = mm(left_root, g).astype(jnp.bfloat16)
    shaped[...] = mm(half, right_root)
    wide = g.astype(jnp.float32)
    grad_norm = jnp.sqrt(jnp.sum(wide * wide))
    whole = shaped[...]
    shaped_norm = jnp.sqrt(jnp.sum(whole * whole) + 1e-06)
    scale = grad_norm / shaped_norm
    own = shaped[:, pl.ds(pl.multiple_of(rep * width, width), width)]
    piece[...] = (own * scale).astype(jnp.bfloat16)
    put_left.wait()
    put_right.wait()


def select_kernel(reps, workers, arrived, out):
    width = arrived.shape[-1]

    @pl.loop(0, out.shape[0] // 8)
    def _(group):
        for k in range(8):
            block = group * 8 + k
            worker = workers[block]
            for part in range(reps):
                out[block, :, part * width : (part + 1) * width] = arrived[part, worker]


def local(gradient, left_stats, right_stats, block_lists, block_counts):
    _, block_total, dev_rows, cols = gradient.shape
    reps, devices = lax.axis_size("rep"), lax.axis_size("fsdp")
    layers = devices // LANES
    width = cols // reps
    rows = devices * dev_rows
    vmem = pl.BlockSpec(memory_space=pltpu.VMEM)
    smem = pl.BlockSpec(memory_space=pltpu.SMEM)
    anywhere = pl.BlockSpec(memory_space=pl.ANY)

    live = block_counts > 0
    ids = jnp.clip(block_lists[:, 0], 0, block_total - 1)
    named = jnp.where(live, block_lists[:, 0], -1)
    place = jnp.arange(devices, dtype=jnp.int32)
    match = named[None, :] == jnp.arange(block_total, dtype=jnp.int32)[:, None]
    workers = jnp.sum(jnp.where(match, place[None, :], 0), axis=1)
    own_live = lax.dynamic_slice_in_dim(block_counts, lax.axis_index("fsdp"), 1)

    slots = jax.ShapeDtypeStruct((reps, layers, LANES, dev_rows, width), jnp.bfloat16)
    blocks = pl.pallas_call(
        functools.partial(gather_kernel, reps, layers),
        out_shape=slots,
        in_specs=[anywhere, smem],
        out_specs=anywhere,
        scratch_shapes=[
            pltpu.VMEM((reps, block_total, dev_rows, width), jnp.bfloat16),
            pltpu.VMEM((block_total, dev_rows, width), jnp.bfloat16),
            pltpu.VMEM((layers, LANES, dev_rows, width), jnp.bfloat16),
            pltpu.SemaphoreType.DMA((reps,)),
            pltpu.SemaphoreType.DMA((reps,)),
            pltpu.SemaphoreType.DMA(()),
        ]
        + exchange_scratch(reps, layers, dev_rows, width),
        compiler_params=pltpu.CompilerParams(
            collective_id=0, has_side_effects=True, vmem_limit_bytes=8 << 20
        ),
        name="gather_blocks",
    )(gradient, ids)

    left_new, right_new, piece = pl.pallas_call(
        functools.partial(block_kernel, reps),
        out_shape=(
            jax.ShapeDtypeStruct(left_stats.shape, jnp.float32),
            jax.ShapeDtypeStruct(right_stats.shape, jnp.float32),
            jax.ShapeDtypeStruct((rows, width), jnp.bfloat16),
        ),
        in_specs=[vmem, vmem, vmem, smem],
        out_specs=(anywhere, anywhere, vmem),
        scratch_shapes=[
            pltpu.VMEM((rows, cols), jnp.bfloat16),
            pltpu.VMEM((rows, rows), jnp.float32),
            pltpu.VMEM((cols, cols), jnp.float32),
            pltpu.VMEM((rows, cols), jnp.float32),
            pltpu.SemaphoreType.DMA((2,)),
        ],
        compiler_params=pltpu.CompilerParams(vmem_limit_bytes=32 << 20),
        name="precondition",
    )(blocks.reshape(reps, rows, width), left_stats, right_stats, own_live)

    arrived = pl.pallas_call(
        functools.partial(return_kernel, reps, layers),
        out_shape=slots,
        in_specs=[anywhere],
        out_specs=anywhere,
        scratch_shapes=exchange_scratch(reps, layers, dev_rows, width),
        compiler_params=pltpu.CompilerParams(
            collective_id=1, has_side_effects=True, vmem_limit_bytes=8 << 20
        ),
        name="return_rows",
    )(piece.reshape(layers, LANES, dev_rows, width))

    direction = pl.pallas_call(
        functools.partial(select_kernel, reps),
        out_shape=jax.ShapeDtypeStruct((block_total, dev_rows, cols), jnp.bfloat16),
        in_specs=[smem, vmem],
        out_specs=vmem,
        name="select_blocks",
    )(workers, arrived.reshape(reps, devices, dev_rows, width))
    return (direction, left_new, right_new)


def solution(mesh):
    placed = (P("rep", None, "fsdp", None), P("fsdp", None, None), P("fsdp", None, None), P(), P())
    return jax.shard_map(
        local,
        mesh=mesh,
        in_specs=placed,
        out_specs=(P(None, "fsdp", None), P("fsdp", None, None), P("fsdp", None, None)),
        check_vma=False,
    )
```

```python
import functools

import jax
import jax.numpy as jnp
from jax import lax
from jax.experimental import pallas as pl
from jax.experimental.pallas import tpu as pltpu
from jax.sharding import PartitionSpec as P

DECAY = 0.95
LANES = 8
MESH = pl.DeviceIdType.MESH
PIECES = 4


def near_first(count):
    order = [0]
    for step in range(1, count // 2 + 1):
        order.append(step)
        if count - step != step:
            order.append(count - step)
    return order


def groups_of(layers):
    cuts = [0, layers]
    return [(lo, hi) for lo, hi in zip(cuts, cuts[1:]) if hi > lo]


def position():
    rep, place = lax.axis_index("rep"), lax.axis_index("fsdp")
    return rep, place, place // LANES, place % LANES


def reach_of(layers):
    return (layers // 2 + 1) // 2


def greet(reps, layers, relay):
    rep, place, layer, lane = position()
    reach = reach_of(layers)
    barrier = pltpu.get_barrier_semaphore()
    peers = []
    for step in range(reach, 0, -1):
        for way in (step, layers - step):
            peers.append((rep, ((layer + way) % layers) * LANES + lane))
    peers += [((rep + turn) % reps, place) for turn in range(1, reps)]
    peers += [(rep, layer * LANES + (lane + hop) % LANES) for hop in range(1, LANES)]
    for peer in peers:
        pl.semaphore_signal(barrier, inc=1, device_id=peer, device_id_type=MESH)
    pl.semaphore_wait(barrier, len(peers))
    for way in (reach, layers - reach):
        there = ((layer + way) % layers) * LANES + lane
        pl.semaphore_signal(relay, inc=1, device_id=(rep, there), device_id_type=MESH)


def take(ref, sem):
    pltpu.make_async_copy(ref, ref, sem).wait()


def exchange(reps, layers, send, mid, out, a_send, a_recv, b_send, b_recv):
    rep, _, layer, lane = position()
    order = near_first(layers)
    groups = groups_of(layers)
    for slot in range(layers - 1, 0, -1):
        there = (layer - order[slot] + layers) % layers
        group = [lo <= slot < hi for lo, hi in groups].index(True)
        pltpu.make_async_remote_copy(
            src_ref=send.at[there],
            dst_ref=mid.at[:, slot],
            send_sem=a_send,
            recv_sem=a_recv.at[group],
            device_id=(rep, there * LANES + lane),
            device_id_type=MESH,
        ).start()
    mid[:, 0] = send[layer]
    for group, (lo, hi) in enumerate(groups):
        if max(lo, 1) < hi:
            take(mid.at[:, max(lo, 1) : hi], a_recv.at[group])
        for turn in [t for t in (2, 1, 3) if t < reps] + [0]:
            for hop in (4, 3, 5, 2, 6, 1, 7, 0):
                if turn or hop:
                    target = (lane + hop) % LANES
                    pltpu.make_async_remote_copy(
                        src_ref=mid.at[target, lo:hi],
                        dst_ref=out.at[rep, lo:hi, lane],
                        send_sem=b_send.at[min(turn, 1)],
                        recv_sem=b_recv.at[min(turn, 1)],
                        device_id=((rep + turn) % reps, layer * LANES + target),
                        device_id_type=MESH,
                    ).start()
    out[rep, :, lane] = mid[lane]
    take(out.at[0 : reps - 1], b_recv.at[1])
    take(out.at[0, 0 : layers - layers // LANES], b_recv.at[0])


def exchange_end(reps, layers, mid, out, a_send, b_send):
    take(mid.at[:, 1:], a_send)
    take(out.at[0 : reps - 1], b_send.at[1])
    take(out.at[0, 0 : layers - layers // LANES], b_send.at[0])


def mm(a, b, dims=((1,), (0,))):
    return lax.dot_general(a, b, (dims, ((), ())), preferred_element_type=jnp.float32)


def root(stat):
    size = stat.shape[0]
    bound = jnp.max(jnp.sum(jnp.abs(stat), axis=0, keepdims=True))
    factor = 2.5 / bound
    row = lax.broadcasted_iota(jnp.int32, (size, size), 0)
    col = lax.broadcasted_iota(jnp.int32, (size, size), 1)
    diagonal = row == col
    d = jnp.where(diagonal, 0.25, 0.0) - (0.25 * factor) * stat
    low = d.astype(jnp.bfloat16)
    e = 2.0 * d + mm(low, low)
    low = e.astype(jnp.bfloat16)
    k = 2.0 * e + mm(low, low)
    j = 5.0 * d - 4.0 * e
    kj = mm(k.astype(jnp.bfloat16), j.astype(jnp.bfloat16))
    gain = jnp.sqrt(jnp.sqrt(factor))
    return (gain * (jnp.where(diagonal, 1.0, 0.0) + e - 0.25 * (k + kj))).astype(jnp.bfloat16)


def kernel(
    reps, layers, grad, ids_in, counts_in, left, right,
    direction, left_out, right_out,
    parts, total, send, mid_in, blocks, g_ref, stat_left, stat_right, left_new, right_new, shaped,
    piece, mid_out, arrived, table, table_smem, ids, counts, ids_row, counts_row,
    relay, r_send, r_recv, r_own, small_sems, stat_sems, put_sems, table_sem,
    a_send, a_recv, b_send, b_recv, c_send, c_recv, d_send, d_recv,
):
    rep, place, layer, lane = position()
    block_total, dev_rows, width = total.shape
    rows = LANES * dev_rows
    greet(reps, layers, relay)

    for turn in [t for t in (2, 1, 3) if t < reps]:
        there = (rep + turn) % reps
        pltpu.make_async_remote_copy(
            src_ref=grad.at[0, :, :, pl.ds(pl.multiple_of(there * width, width), width)],
            dst_ref=parts.at[turn],
            send_sem=r_send,
            recv_sem=r_recv,
            device_id=(there, place),
            device_id_type=MESH,
        ).start()

    mine = pltpu.make_async_copy(
        grad.at[0, :, :, pl.ds(pl.multiple_of(rep * width, width), width)], parts.at[0], r_own
    )
    small = [
        pltpu.make_async_copy(ids_in, ids, small_sems.at[0]),
        pltpu.make_async_copy(counts_in, counts, small_sems.at[1]),
        pltpu.make_async_copy(ids_in, ids_row, small_sems.at[2]),
        pltpu.make_async_copy(counts_in, counts_row, small_sems.at[3]),
    ]
    get_left = pltpu.make_async_copy(left.at[0], stat_left, stat_sems.at[0])
    get_right = pltpu.make_async_copy(right.at[0], stat_right, stat_sems.at[1])
    for copy in (mine, *small, get_left, get_right):
        copy.start()
    for copy in small:
        copy.wait()

    devices = layers * LANES
    worker = lax.broadcasted_iota(jnp.int32, (devices, devices), 0)
    named = jnp.where(counts_row[...] > 0, ids_row[...], -1)
    named = jnp.transpose(jnp.broadcast_to(named, (devices, devices)))
    match = named == lax.broadcasted_iota(jnp.int32, (devices, devices), 1)
    offset = (worker // LANES - layer + layers) % layers
    slot = jnp.where(offset <= layers // 2, jnp.maximum(2 * offset - 1, 0), 2 * (layers - offset))
    spot = slot * LANES + worker % LANES
    table[...] = jnp.max(jnp.where(match, spot, 0), axis=0, keepdims=True)
    put_table = pltpu.make_async_copy(table, table_smem, table_sem)
    put_table.start()

    mine.wait()
    take(parts.at[1:reps], r_recv)
    acc = parts[0].astype(jnp.float32)
    for turn in range(1, reps):
        acc = acc + parts[turn].astype(jnp.float32)
    total[...] = acc.astype(jnp.bfloat16)

    @pl.loop(0, layers)
    def _(z):
        for l in range(LANES):
            block = jnp.clip(ids[0, z * LANES + l], 0, block_total - 1)
            send[z, l] = total[block]

    pl.semaphore_wait(relay, 2)
    exchange(reps, layers, send, mid_in, blocks, a_send, a_recv, b_send, b_recv)

    for part in range(reps):
        for slot_at, offset_at in enumerate(near_first(layers)):
            start = pl.multiple_of(((layer + offset_at) % layers) * rows, rows)
            g_ref[pl.ds(start, rows), part * width : (part + 1) * width] = blocks[
                part, slot_at
            ].reshape(rows, width)
    g = g_ref[...]
    used = counts[0, place] > 0
    get_left.wait()
    get_right.wait()
    old = stat_left[...]
    left_new[...] = jnp.where(used, DECAY * old + (1.0 - DECAY) * mm(g, g, ((1,), (1,))), old)
    put_left = pltpu.make_async_copy(left_new, left_out.at[0], put_sems.at[0])
    put_left.start()
    old = stat_right[...]
    right_new[...] = jnp.where(used, DECAY * old + (1.0 - DECAY) * mm(g, g, ((0,), (0,))), old)
    put_right = pltpu.make_async_copy(right_new, right_out.at[0], put_sems.at[1])
    put_right.start()
    left_root = root(left_new[...])
    right_root = root(right_new[...])
    half = mm(left_root, g).astype(jnp.bfloat16)
    shaped[...] = mm(half, right_root)
    wide = g.astype(jnp.float32)
    grad_norm = jnp.sqrt(jnp.sum(wide * wide))
    whole = shaped[...]
    shaped_norm = jnp.sqrt(jnp.sum(whole * whole) + 1e-06)
    own = shaped[:, pl.ds(pl.multiple_of(rep * width, width), width)]
    grafted = (own * (grad_norm / shaped_norm)).astype(jnp.bfloat16)
    piece[...] = grafted.reshape(piece.shape)

    exchange(reps, layers, piece, mid_out, arrived, c_send, c_recv, d_send, d_recv)
    put_table.wait()

    @pl.loop(0, block_total // 8)
    def _(group):
        for k in range(8):
            block = group * 8 + k
            spot_at = table_smem[0, block]
            for part in range(reps):
                direction[block, :, part * width : (part + 1) * width] = arrived[
                    part, spot_at // LANES, spot_at % LANES
                ]

    take(parts.at[1:reps], r_send)
    exchange_end(reps, layers, mid_in, blocks, a_send, b_send)
    exchange_end(reps, layers, mid_out, arrived, c_send, d_send)
    put_left.wait()
    put_right.wait()


def hand_over(direction, left, right, direction_out, left_out, right_out, a, b, c, get_sems, put_sems):
    moves = []
    for k, (src, via, dst) in enumerate(
        [(left.at[0], a, left_out.at[0]), (right.at[0], b, right_out.at[0]), (direction, c, direction_out)]
    ):
        step = src.shape[0] // PIECES
        for p in range(PIECES):
            span = pl.ds(p * step, step)
            moves.append(
                (
                    pltpu.make_async_copy(src.at[span], via.at[span], get_sems.at[k, p]),
                    pltpu.make_async_copy(via.at[span], dst.at[span], put_sems.at[k, p]),
                )
            )
    for get, _ in moves:
        get.start()
    for get, put in moves:
        get.wait()
        put.start()
    for _, put in moves:
        put.wait()


def local(gradient, left_stats, right_stats, block_lists, block_counts):
    _, block_total, dev_rows, cols = gradient.shape
    reps, devices = lax.axis_size("rep"), lax.axis_size("fsdp")
    layers = devices // LANES
    width = cols // reps
    rows = devices * dev_rows
    vmem = pl.BlockSpec(memory_space=pltpu.VMEM)
    anywhere = pl.BlockSpec(memory_space=pl.ANY)
    groups = len(groups_of(layers))
    direction, left_new, right_new = pl.pallas_call(
        functools.partial(kernel, reps, layers),
        out_shape=(
            jax.ShapeDtypeStruct((block_total, dev_rows, cols), jnp.bfloat16),
            jax.ShapeDtypeStruct(left_stats.shape, jnp.float32),
            jax.ShapeDtypeStruct(right_stats.shape, jnp.float32),
        ),
        in_specs=[anywhere] * 5,
        out_specs=(vmem, anywhere, anywhere),
        scratch_shapes=[
            pltpu.VMEM((reps, block_total, dev_rows, width), jnp.bfloat16),
            pltpu.VMEM((block_total, dev_rows, width), jnp.bfloat16),
            pltpu.VMEM((layers, LANES, dev_rows, width), jnp.bfloat16),
            pltpu.VMEM((LANES, layers, dev_rows, width), jnp.bfloat16),
            pltpu.VMEM((reps, layers, LANES, dev_rows, width), jnp.bfloat16),
            pltpu.VMEM((rows, cols), jnp.bfloat16),
            pltpu.VMEM((rows, rows), jnp.float32),
            pltpu.VMEM((cols, cols), jnp.float32),
            pltpu.VMEM((rows, rows), jnp.float32),
            pltpu.VMEM((cols, cols), jnp.float32),
            pltpu.VMEM((rows, cols), jnp.float32),
            pltpu.VMEM((layers, LANES, dev_rows, width), jnp.bfloat16),
            pltpu.VMEM((LANES, layers, dev_rows, width), jnp.bfloat16),
            pltpu.VMEM((reps, layers, LANES, dev_rows, width), jnp.bfloat16),
            pltpu.VMEM((1, devices), jnp.int32),
            pltpu.SMEM((1, devices), jnp.int32),
            pltpu.SMEM((1, devices), jnp.int32),
            pltpu.SMEM((1, devices), jnp.int32),
            pltpu.VMEM((1, devices), jnp.int32),
            pltpu.VMEM((1, devices), jnp.int32),
            pltpu.SemaphoreType.REGULAR,
            pltpu.SemaphoreType.DMA(()),
            pltpu.SemaphoreType.DMA(()),
            pltpu.SemaphoreType.DMA(()),
            pltpu.SemaphoreType.DMA((4,)),
            pltpu.SemaphoreType.DMA((2,)),
            pltpu.SemaphoreType.DMA((2,)),
            pltpu.SemaphoreType.DMA(()),
        ]
        + 2
        * [
            pltpu.SemaphoreType.DMA(()),
            pltpu.SemaphoreType.DMA((groups,)),
            pltpu.SemaphoreType.DMA((2,)),
            pltpu.SemaphoreType.DMA((2,)),
        ],
        compiler_params=pltpu.CompilerParams(
            collective_id=0, has_side_effects=True, vmem_limit_bytes=63 << 20
        ),
        name="shampoo_step",
    )(
        gradient, block_lists.reshape(1, devices), block_counts.reshape(1, devices),
        left_stats, right_stats,
    )
    results = (direction, left_new, right_new)
    return pl.pallas_call(
        hand_over,
        out_shape=tuple(jax.ShapeDtypeStruct(x.shape, x.dtype) for x in results),
        in_specs=[anywhere] * 3,
        out_specs=(anywhere,) * 3,
        scratch_shapes=[
            pltpu.VMEM(left_stats.shape[1:], jnp.float32),
            pltpu.VMEM(right_stats.shape[1:], jnp.float32),
            pltpu.VMEM(direction.shape, jnp.bfloat16),
            pltpu.SemaphoreType.DMA((3, PIECES)),
            pltpu.SemaphoreType.DMA((3, PIECES)),
        ],
        compiler_params=pltpu.CompilerParams(vmem_limit_bytes=63 << 20),
        name="hand_over",
    )(*results)


def solution(mesh):
    placed = (P("rep", None, "fsdp", None), P("fsdp", None, None), P("fsdp", None, None), P(), P())
    return jax.shard_map(
        local,
        mesh=mesh,
        in_specs=placed,
        out_specs=(P(None, "fsdp", None), P("fsdp", None, None), P("fsdp", None, None)),
        check_vma=False,
    )
```

```python
import functools

import jax
import jax.numpy as jnp
from jax import lax
from jax.experimental import pallas as pl
from jax.experimental.pallas import tpu as pltpu
from jax.sharding import PartitionSpec as P

DECAY = 0.95
LANES = 8
MESH = pl.DeviceIdType.MESH
PIECES = 2
GROUPS = 4


def near_first(count):
    order = [0]
    for step in range(1, count // 2 + 1):
        order.append(step)
        if count - step != step:
            order.append(count - step)
    return order


def groups_of(layers, cuts):
    ends = [0] + [cut * layers // 16 for cut in cuts] + [layers]
    return [(lo, hi) for lo, hi in zip(ends, ends[1:]) if hi > lo]


def position():
    rep, place = lax.axis_index("rep"), lax.axis_index("fsdp")
    return rep, place, place // LANES, place % LANES


def reach_of(layers):
    return (layers // 2 + 1) // 2


def greet(reps, layers, relay):
    rep, place, layer, lane = position()
    reach = reach_of(layers)
    barrier = pltpu.get_barrier_semaphore()
    peers = []
    for step in range(reach, 0, -1):
        for way in (step, layers - step):
            peers.append((rep, ((layer + way) % layers) * LANES + lane))
    peers += [((rep + turn) % reps, place) for turn in range(1, reps)]
    peers += [(rep, layer * LANES + (lane + hop) % LANES) for hop in range(1, LANES)]
    for peer in peers:
        pl.semaphore_signal(barrier, inc=1, device_id=peer, device_id_type=MESH)
    pl.semaphore_wait(barrier, len(peers))
    for way in (reach, layers - reach):
        there = ((layer + way) % layers) * LANES + lane
        pl.semaphore_signal(relay, inc=1, device_id=(rep, there), device_id_type=MESH)


def take(ref, sem):
    pltpu.make_async_copy(ref, ref, sem).wait()


def exchange(reps, layers, cuts, send, mid, out, a_send, a_recv, b_send, b_recv):
    rep, _, layer, lane = position()
    order = near_first(layers)
    groups = groups_of(layers, cuts)
    for slot in range(1, layers) if cuts else range(layers - 1, 0, -1):
        there = (layer - order[slot] + layers) % layers
        group = [lo <= slot < hi for lo, hi in groups].index(True)
        pltpu.make_async_remote_copy(
            src_ref=send.at[there],
            dst_ref=mid.at[:, slot],
            send_sem=a_send,
            recv_sem=a_recv.at[group],
            device_id=(rep, there * LANES + lane),
            device_id_type=MESH,
        ).start()
    mid[:, 0] = send[layer]
    for group, (lo, hi) in enumerate(groups):
        if max(lo, 1) < hi:
            take(mid.at[:, max(lo, 1) : hi], a_recv.at[group])
        for turn in [t for t in (2, 1, 3) if t < reps] + [0]:
            for hop in (4, 3, 5, 2, 6, 1, 7, 0):
                if turn or hop:
                    target = (lane + hop) % LANES
                    pltpu.make_async_remote_copy(
                        src_ref=mid.at[target, lo:hi],
                        dst_ref=out.at[rep, lo:hi, lane],
                        send_sem=b_send.at[min(turn, 1)],
                        recv_sem=b_recv.at[min(turn, 1)],
                        device_id=((rep + turn) % reps, layer * LANES + target),
                        device_id_type=MESH,
                    ).start()
    out[rep, :, lane] = mid[lane]
    take(out.at[0 : reps - 1], b_recv.at[1])
    take(out.at[0, 0 : layers - layers // LANES], b_recv.at[0])


def exchange_end(reps, layers, mid, out, a_send, b_send):
    take(mid.at[:, 1:], a_send)
    take(out.at[0 : reps - 1], b_send.at[1])
    take(out.at[0, 0 : layers - layers // LANES], b_send.at[0])


def mm(a, b, dims=((1,), (0,))):
    return lax.dot_general(a, b, (dims, ((), ())), preferred_element_type=jnp.float32)


def root(stat):
    size = stat.shape[0]
    bound = jnp.max(jnp.sum(jnp.abs(stat), axis=0, keepdims=True))
    factor = 2.5 / bound
    row = lax.broadcasted_iota(jnp.int32, (size, size), 0)
    col = lax.broadcasted_iota(jnp.int32, (size, size), 1)
    diagonal = row == col
    d = jnp.where(diagonal, 0.25, 0.0) - (0.25 * factor) * stat
    low = d.astype(jnp.bfloat16)
    e = 2.0 * d + mm(low, low)
    low = e.astype(jnp.bfloat16)
    k = 2.0 * e + mm(low, low)
    j = 5.0 * d - 4.0 * e
    kj = mm(k.astype(jnp.bfloat16), j.astype(jnp.bfloat16))
    gain = jnp.sqrt(jnp.sqrt(factor))
    return (gain * (jnp.where(diagonal, 1.0, 0.0) + e - 0.25 * (k + kj))).astype(jnp.bfloat16)


def kernel(
    reps, layers, grad, ids_in, counts_in, left, right,
    direction, left_out, right_out,
    local, parts, total, send, mid_in, blocks, g_ref, stat_left, stat_right, left_new, right_new, shaped,
    piece, mid_out, arrived, table, table_smem, ids, counts, ids_row, counts_row,
    relay, r_send, r_recv, fetch_sems, small_sems, stat_sems, put_sems, table_sem,
    a_send, a_recv, b_send, b_recv, c_send, c_recv, d_send, d_recv,
):
    rep, place, layer, lane = position()
    block_total, dev_rows, width = total.shape
    rows = LANES * dev_rows
    fetch = []
    for part in range(reps):
        fetch.append(
            pltpu.make_async_copy(
                grad.at[0, :, :, part * width : (part + 1) * width], local.at[part], fetch_sems.at[part]
            )
        )
        fetch[-1].start()
    greet(reps, layers, relay)
    for copy in fetch:
        copy.wait()

    for turn in [t for t in (2, 1, 3) if t < reps]:
        there = (rep + turn) % reps
        pltpu.make_async_remote_copy(
            src_ref=local.at[there],
            dst_ref=parts.at[turn],
            send_sem=r_send,
            recv_sem=r_recv,
            device_id=(there, place),
            device_id_type=MESH,
        ).start()

    small = [
        pltpu.make_async_copy(ids_in, ids, small_sems.at[0]),
        pltpu.make_async_copy(counts_in, counts, small_sems.at[1]),
        pltpu.make_async_copy(ids_in, ids_row, small_sems.at[2]),
        pltpu.make_async_copy(counts_in, counts_row, small_sems.at[3]),
    ]
    get_left = pltpu.make_async_copy(left.at[0], stat_left, stat_sems.at[0])
    get_right = pltpu.make_async_copy(right.at[0], stat_right, stat_sems.at[1])
    for copy in (*small, get_left, get_right):
        copy.start()
    for copy in small:
        copy.wait()

    devices = layers * LANES
    worker = lax.broadcasted_iota(jnp.int32, (devices, devices), 0)
    named = jnp.where(counts_row[...] > 0, ids_row[...], -1)
    named = jnp.transpose(jnp.broadcast_to(named, (devices, devices)))
    match = named == lax.broadcasted_iota(jnp.int32, (devices, devices), 1)
    offset = (worker // LANES - layer + layers) % layers
    slot = jnp.where(offset <= layers // 2, jnp.maximum(2 * offset - 1, 0), 2 * (layers - offset))
    spot = slot * LANES + worker % LANES
    table[...] = jnp.max(jnp.where(match, spot, 0), axis=0, keepdims=True)
    put_table = pltpu.make_async_copy(table, table_smem, table_sem)
    put_table.start()

    take(parts.at[1:reps], r_recv)
    acc = local[rep].astype(jnp.float32)
    for turn in range(1, reps):
        acc = acc + parts[turn].astype(jnp.float32)
    total[...] = acc.astype(jnp.bfloat16)

    @pl.loop(0, layers)
    def _(z):
        for l in range(LANES):
            block = jnp.clip(ids[0, z * LANES + l], 0, block_total - 1)
            send[z, l] = total[block]

    pl.semaphore_wait(relay, 2)
    exchange(reps, layers, (), send, mid_in, blocks, a_send, a_recv, b_send, b_recv)

    for part in range(reps):
        for slot_at, offset_at in enumerate(near_first(layers)):
            start = pl.multiple_of(((layer + offset_at) % layers) * rows, rows)
            g_ref[pl.ds(start, rows), part * width : (part + 1) * width] = blocks[
                part, slot_at
            ].reshape(rows, width)
    g = g_ref[...]
    used = counts[0, place] > 0
    get_left.wait()
    get_right.wait()
    old = stat_left[...]
    left_new[...] = jnp.where(used, DECAY * old + (1.0 - DECAY) * mm(g, g, ((1,), (1,))), old)
    left_out[0] = left_new[...]
    old = stat_right[...]
    right_new[...] = jnp.where(used, DECAY * old + (1.0 - DECAY) * mm(g, g, ((0,), (0,))), old)
    right_out[0] = right_new[...]
    left_root = root(left_new[...])
    right_root = root(right_new[...])
    half = mm(left_root, g).astype(jnp.bfloat16)
    shaped[...] = mm(half, right_root)
    wide = g.astype(jnp.float32)
    grad_norm = jnp.sqrt(jnp.sum(wide * wide))
    whole = shaped[...]
    shaped_norm = jnp.sqrt(jnp.sum(whole * whole) + 1e-06)
    own = shaped[:, pl.ds(pl.multiple_of(rep * width, width), width)]
    grafted = (own * (grad_norm / shaped_norm)).astype(jnp.bfloat16)
    piece[...] = grafted.reshape(piece.shape)

    exchange(reps, layers, (7,), piece, mid_out, arrived, c_send, c_recv, d_send, d_recv)
    put_table.wait()

    @pl.loop(0, block_total // 8)
    def _(group):
        for k in range(8):
            block = group * 8 + k
            spot_at = table_smem[0, block]
            for part in range(reps):
                direction[block, :, part * width : (part + 1) * width] = arrived[
                    part, spot_at // LANES, spot_at % LANES
                ]

    take(parts.at[1:reps], r_send)
    exchange_end(reps, layers, mid_in, blocks, a_send, b_send)
    exchange_end(reps, layers, mid_out, arrived, c_send, d_send)


def hand_over(direction, left, right, direction_out, left_out, right_out, sems):
    copies = []
    for k, (src, dst) in enumerate(
        [(left.at[0], left_out.at[0]), (right.at[0], right_out.at[0]), (direction, direction_out)]
    ):
        step = src.shape[0] // PIECES
        for p in range(PIECES):
            span = pl.ds(p * step, step)
            copies.append(pltpu.make_async_copy(src.at[span], dst.at[span], sems.at[k, p]))
    for copy in copies:
        copy.start()
    for copy in copies:
        copy.wait()


def local(gradient, left_stats, right_stats, block_lists, block_counts):
    _, block_total, dev_rows, cols = gradient.shape
    reps, devices = lax.axis_size("rep"), lax.axis_size("fsdp")
    layers = devices // LANES
    width = cols // reps
    rows = devices * dev_rows
    vmem = pl.BlockSpec(memory_space=pltpu.VMEM)
    anywhere = pl.BlockSpec(memory_space=pl.ANY)
    def keep(x):
        return pltpu.with_memory_space_constraint(x, pltpu.HBM)

    direction, left_new, right_new = pl.pallas_call(
        functools.partial(kernel, reps, layers),
        out_shape=(
            pltpu.VMEM((block_total, dev_rows, cols), jnp.bfloat16),
            pltpu.VMEM(left_stats.shape, jnp.float32),
            pltpu.VMEM(right_stats.shape, jnp.float32),
        ),
        in_specs=[anywhere] * 5,
        out_specs=(vmem, vmem, vmem),
        scratch_shapes=[
            pltpu.VMEM((reps, block_total, dev_rows, width), jnp.bfloat16),
            pltpu.VMEM((reps, block_total, dev_rows, width), jnp.bfloat16),
            pltpu.VMEM((block_total, dev_rows, width), jnp.bfloat16),
            pltpu.VMEM((layers, LANES, dev_rows, width), jnp.bfloat16),
            pltpu.VMEM((LANES, layers, dev_rows, width), jnp.bfloat16),
            pltpu.VMEM((reps, layers, LANES, dev_rows, width), jnp.bfloat16),
            pltpu.VMEM((rows, cols), jnp.bfloat16),
            pltpu.VMEM((rows, rows), jnp.float32),
            pltpu.VMEM((cols, cols), jnp.float32),
            pltpu.VMEM((rows, rows), jnp.float32),
            pltpu.VMEM((cols, cols), jnp.float32),
            pltpu.VMEM((rows, cols), jnp.float32),
            pltpu.VMEM((layers, LANES, dev_rows, width), jnp.bfloat16),
            pltpu.VMEM((LANES, layers, dev_rows, width), jnp.bfloat16),
            pltpu.VMEM((reps, layers, LANES, dev_rows, width), jnp.bfloat16),
            pltpu.VMEM((1, devices), jnp.int32),
            pltpu.SMEM((1, devices), jnp.int32),
            pltpu.SMEM((1, devices), jnp.int32),
            pltpu.SMEM((1, devices), jnp.int32),
            pltpu.VMEM((1, devices), jnp.int32),
            pltpu.VMEM((1, devices), jnp.int32),
            pltpu.SemaphoreType.REGULAR,
            pltpu.SemaphoreType.DMA(()),
            pltpu.SemaphoreType.DMA(()),
            pltpu.SemaphoreType.DMA((reps,)),
            pltpu.SemaphoreType.DMA((4,)),
            pltpu.SemaphoreType.DMA((2,)),
            pltpu.SemaphoreType.DMA((2,)),
            pltpu.SemaphoreType.DMA(()),
        ]
        + 2
        * [
            pltpu.SemaphoreType.DMA(()),
            pltpu.SemaphoreType.DMA((GROUPS,)),
            pltpu.SemaphoreType.DMA((2,)),
            pltpu.SemaphoreType.DMA((2,)),
        ],
        compiler_params=pltpu.CompilerParams(
            collective_id=0, has_side_effects=True, vmem_limit_bytes=40 << 20
        ),
        name="shampoo_step",
    )(
        keep(gradient), keep(block_lists.reshape(1, devices)), keep(block_counts.reshape(1, devices)),
        keep(left_stats), keep(right_stats),
    )
    results = (direction, left_new, right_new)
    return pl.pallas_call(
        hand_over,
        out_shape=tuple(jax.ShapeDtypeStruct(x.shape, x.dtype) for x in results),
        in_specs=[pl.BlockSpec(memory_space=pltpu.VMEM)] * 3,
        out_specs=(anywhere,) * 3,
        scratch_shapes=[pltpu.SemaphoreType.DMA((3, PIECES))],
        compiler_params=pltpu.CompilerParams(vmem_limit_bytes=16 << 20),
        name="hand_over",
    )(*results)


def solution(mesh):
    placed = (P("rep", None, "fsdp", None), P("fsdp", None, None), P("fsdp", None, None), P(), P())
    return jax.shard_map(
        local,
        mesh=mesh,
        in_specs=placed,
        out_specs=(P(None, "fsdp", None), P("fsdp", None, None), P("fsdp", None, None)),
        check_vma=False,
    )
```

```python
import functools

import jax
import jax.numpy as jnp
from jax import lax
from jax.experimental import pallas as pl
from jax.experimental.pallas import tpu as pltpu
from jax.sharding import PartitionSpec as P

DECAY = 0.95
LANES = 8
MESH = pl.DeviceIdType.MESH
PIECES = 2
GROUPS = 4


def near_first(count):
    order = [0]
    for step in range(1, count // 2 + 1):
        order.append(step)
        if count - step != step:
            order.append(count - step)
    return order


def groups_of(layers, cuts):
    ends = [0] + [cut * layers // 16 for cut in cuts] + [layers]
    return [(lo, hi) for lo, hi in zip(ends, ends[1:]) if hi > lo]


def position():
    rep, place = lax.axis_index("rep"), lax.axis_index("fsdp")
    return rep, place, place // LANES, place % LANES


def reach_of(layers):
    return (layers // 2 + 1) // 2


def greet(reps, layers, relay):
    rep, place, layer, lane = position()
    reach = reach_of(layers)
    barrier = pltpu.get_barrier_semaphore()
    peers = []
    for step in range(reach, 0, -1):
        for way in (step, layers - step):
            peers.append((rep, ((layer + way) % layers) * LANES + lane))
    peers += [((rep + turn) % reps, place) for turn in range(1, reps)]
    peers += [(rep, layer * LANES + (lane + hop) % LANES) for hop in range(1, LANES)]
    for peer in peers:
        pl.semaphore_signal(barrier, inc=1, device_id=peer, device_id_type=MESH)
    pl.semaphore_wait(barrier, len(peers))
    for way in (reach, layers - reach):
        there = ((layer + way) % layers) * LANES + lane
        pl.semaphore_signal(relay, inc=1, device_id=(rep, there), device_id_type=MESH)


def take(ref, sem):
    pltpu.make_async_copy(ref, ref, sem).wait()


def exchange(reps, layers, cuts, order_a, send, mid, out, a_send, a_recv, b_send, b_recv):
    rep, _, layer, lane = position()
    order = near_first(layers)
    groups = groups_of(layers, cuts)
    for slot in order_a:
        there = (layer - order[slot] + layers) % layers
        group = [lo <= slot < hi for lo, hi in groups].index(True)
        pltpu.make_async_remote_copy(
            src_ref=send.at[there],
            dst_ref=mid.at[:, slot],
            send_sem=a_send,
            recv_sem=a_recv.at[group],
            device_id=(rep, there * LANES + lane),
            device_id_type=MESH,
        ).start()
    mid[:, 0] = send[layer]
    for group, (lo, hi) in enumerate(groups):
        if max(lo, 1) < hi:
            take(mid.at[:, max(lo, 1) : hi], a_recv.at[group])
        for turn in [t for t in (2, 1, 3) if t < reps] + [0]:
            for hop in (4, 6, 2, 5, 3, 7, 1, 0):
                if turn or hop:
                    target = (lane + hop) % LANES
                    pltpu.make_async_remote_copy(
                        src_ref=mid.at[target, lo:hi],
                        dst_ref=out.at[rep, lo:hi, lane],
                        send_sem=b_send.at[min(turn, 1)],
                        recv_sem=b_recv.at[min(turn, 1)],
                        device_id=((rep + turn) % reps, layer * LANES + target),
                        device_id_type=MESH,
                    ).start()
    out[rep, :, lane] = mid[lane]
    take(out.at[0 : reps - 1], b_recv.at[1])
    take(out.at[0, 0 : layers - layers // LANES], b_recv.at[0])


def exchange_end(reps, layers, mid, out, a_send, b_send):
    take(mid.at[:, 1:], a_send)
    take(out.at[0 : reps - 1], b_send.at[1])
    take(out.at[0, 0 : layers - layers // LANES], b_send.at[0])


def mm(a, b, dims=((1,), (0,))):
    return lax.dot_general(a, b, (dims, ((), ())), preferred_element_type=jnp.float32)


def root(stat):
    size = stat.shape[0]
    bound = jnp.max(jnp.sum(jnp.abs(stat), axis=0, keepdims=True))
    factor = 2.5 / bound
    row = lax.broadcasted_iota(jnp.int32, (size, size), 0)
    col = lax.broadcasted_iota(jnp.int32, (size, size), 1)
    diagonal = row == col
    d = jnp.where(diagonal, 0.25, 0.0) - (0.25 * factor) * stat
    low = d.astype(jnp.bfloat16)
    e = 2.0 * d + mm(low, low)
    low = e.astype(jnp.bfloat16)
    k = 2.0 * e + mm(low, low)
    j = 5.0 * d - 4.0 * e
    kj = mm(k.astype(jnp.bfloat16), j.astype(jnp.bfloat16))
    gain = jnp.sqrt(jnp.sqrt(factor))
    return (gain * (jnp.where(diagonal, 1.0, 0.0) + e - 0.25 * (k + kj))).astype(jnp.bfloat16)


def kernel(
    reps, layers, grad, ids_in, counts_in, left, right,
    direction, left_out, right_out,
    local, parts, total, send, mid_in, blocks, g_ref, stat_left, stat_right, left_new, right_new, shaped,
    piece, mid_out, arrived, table, table_smem, ids, counts, ids_row, counts_row,
    relay, r_send, r_recv, fetch_sems, small_sems, stat_sems, put_sems, table_sem,
    a_send, a_recv, b_send, b_recv, c_send, c_recv, d_send, d_recv,
):
    rep, place, layer, lane = position()
    block_total, dev_rows, width = total.shape
    rows = LANES * dev_rows
    fetch = []
    for part in range(reps):
        fetch.append(
            pltpu.make_async_copy(
                grad.at[0, :, :, part * width : (part + 1) * width], local.at[part], fetch_sems.at[part]
            )
        )
        fetch[-1].start()
    greet(reps, layers, relay)
    for copy in fetch:
        copy.wait()

    for turn in [t for t in (2, 1, 3) if t < reps]:
        there = (rep + turn) % reps
        pltpu.make_async_remote_copy(
            src_ref=local.at[there],
            dst_ref=parts.at[turn],
            send_sem=r_send,
            recv_sem=r_recv,
            device_id=(there, place),
            device_id_type=MESH,
        ).start()

    small = [
        pltpu.make_async_copy(ids_in, ids, small_sems.at[0]),
        pltpu.make_async_copy(counts_in, counts, small_sems.at[1]),
        pltpu.make_async_copy(ids_in, ids_row, small_sems.at[2]),
        pltpu.make_async_copy(counts_in, counts_row, small_sems.at[3]),
    ]
    get_left = pltpu.make_async_copy(left.at[0], stat_left, stat_sems.at[0])
    get_right = pltpu.make_async_copy(right.at[0], stat_right, stat_sems.at[1])
    for copy in (*small, get_left, get_right):
        copy.start()
    for copy in small:
        copy.wait()

    devices = layers * LANES
    worker = lax.broadcasted_iota(jnp.int32, (devices, devices), 0)
    named = jnp.where(counts_row[...] > 0, ids_row[...], -1)
    named = jnp.transpose(jnp.broadcast_to(named, (devices, devices)))
    match = named == lax.broadcasted_iota(jnp.int32, (devices, devices), 1)
    offset = (worker // LANES - layer + layers) % layers
    slot = jnp.where(offset <= layers // 2, jnp.maximum(2 * offset - 1, 0), 2 * (layers - offset))
    spot = slot * LANES + worker % LANES
    table[...] = jnp.max(jnp.where(match, spot, 0), axis=0, keepdims=True)
    put_table = pltpu.make_async_copy(table, table_smem, table_sem)
    put_table.start()

    take(parts.at[1:reps], r_recv)
    acc = local[rep].astype(jnp.float32)
    for turn in range(1, reps):
        acc = acc + parts[turn].astype(jnp.float32)
    total[...] = acc.astype(jnp.bfloat16)

    @pl.loop(0, layers)
    def _(z):
        for l in range(LANES):
            block = jnp.clip(ids[0, z * LANES + l], 0, block_total - 1)
            send[z, l] = total[block]

    pl.semaphore_wait(relay, 2)
    far_first = range(layers - 1, 0, -1)
    exchange(reps, layers, (3,), far_first, send, mid_in, blocks, a_send, a_recv, b_send, b_recv)

    for part in range(reps):
        for slot_at, offset_at in enumerate(near_first(layers)):
            start = pl.multiple_of(((layer + offset_at) % layers) * rows, rows)
            g_ref[pl.ds(start, rows), part * width : (part + 1) * width] = blocks[
                part, slot_at
            ].reshape(rows, width)
    g = g_ref[...]
    used = counts[0, place] > 0
    get_left.wait()
    get_right.wait()
    old = stat_left[...]
    left_new[...] = jnp.where(used, DECAY * old + (1.0 - DECAY) * mm(g, g, ((1,), (1,))), old)
    left_out[0] = left_new[...]
    old = stat_right[...]
    right_new[...] = jnp.where(used, DECAY * old + (1.0 - DECAY) * mm(g, g, ((0,), (0,))), old)
    right_out[0] = right_new[...]
    left_root = root(left_new[...])
    right_root = root(right_new[...])
    half = mm(left_root, g).astype(jnp.bfloat16)
    shaped[...] = mm(half, right_root)
    wide = g.astype(jnp.float32)
    grad_norm = jnp.sqrt(jnp.sum(wide * wide))
    whole = shaped[...]
    shaped_norm = jnp.sqrt(jnp.sum(whole * whole) + 1e-06)
    own = shaped[:, pl.ds(pl.multiple_of(rep * width, width), width)]
    grafted = (own * (grad_norm / shaped_norm)).astype(jnp.bfloat16)
    piece[...] = grafted.reshape(piece.shape)

    exchange(reps, layers, (5, 11), range(1, layers), piece, mid_out, arrived, c_send, c_recv, d_send, d_recv)
    put_table.wait()

    @pl.loop(0, block_total // 8)
    def _(group):
        for k in range(8):
            block = group * 8 + k
            spot_at = table_smem[0, block]
            for part in range(reps):
                direction[block, :, part * width : (part + 1) * width] = arrived[
                    part, spot_at // LANES, spot_at % LANES
                ]

    take(parts.at[1:reps], r_send)
    exchange_end(reps, layers, mid_in, blocks, a_send, b_send)
    exchange_end(reps, layers, mid_out, arrived, c_send, d_send)


def hand_over(direction, left, right, direction_out, left_out, right_out, sems):
    copies = []
    for k, (src, dst) in enumerate(
        [(left.at[0], left_out.at[0]), (right.at[0], right_out.at[0]), (direction, direction_out)]
    ):
        step = src.shape[0] // PIECES
        for p in range(PIECES):
            span = pl.ds(p * step, step)
            copies.append(pltpu.make_async_copy(src.at[span], dst.at[span], sems.at[k, p]))
    for copy in copies:
        copy.start()
    for copy in copies:
        copy.wait()


def local(gradient, left_stats, right_stats, block_lists, block_counts):
    _, block_total, dev_rows, cols = gradient.shape
    reps, devices = lax.axis_size("rep"), lax.axis_size("fsdp")
    layers = devices // LANES
    width = cols // reps
    rows = devices * dev_rows
    vmem = pl.BlockSpec(memory_space=pltpu.VMEM)
    anywhere = pl.BlockSpec(memory_space=pl.ANY)
    def keep(x):
        return pltpu.with_memory_space_constraint(x, pltpu.HBM)

    direction, left_new, right_new = pl.pallas_call(
        functools.partial(kernel, reps, layers),
        out_shape=(
            pltpu.VMEM((block_total, dev_rows, cols), jnp.bfloat16),
            pltpu.VMEM(left_stats.shape, jnp.float32),
            pltpu.VMEM(right_stats.shape, jnp.float32),
        ),
        in_specs=[anywhere] * 5,
        out_specs=(vmem, vmem, vmem),
        scratch_shapes=[
            pltpu.VMEM((reps, block_total, dev_rows, width), jnp.bfloat16),
            pltpu.VMEM((reps, block_total, dev_rows, width), jnp.bfloat16),
            pltpu.VMEM((block_total, dev_rows, width), jnp.bfloat16),
            pltpu.VMEM((layers, LANES, dev_rows, width), jnp.bfloat16),
            pltpu.VMEM((LANES, layers, dev_rows, width), jnp.bfloat16),
            pltpu.VMEM((reps, layers, LANES, dev_rows, width), jnp.bfloat16),
            pltpu.VMEM((rows, cols), jnp.bfloat16),
            pltpu.VMEM((rows, rows), jnp.float32),
            pltpu.VMEM((cols, cols), jnp.float32),
            pltpu.VMEM((rows, rows), jnp.float32),
            pltpu.VMEM((cols, cols), jnp.float32),
            pltpu.VMEM((rows, cols), jnp.float32),
            pltpu.VMEM((layers, LANES, dev_rows, width), jnp.bfloat16),
            pltpu.VMEM((LANES, layers, dev_rows, width), jnp.bfloat16),
            pltpu.VMEM((reps, layers, LANES, dev_rows, width), jnp.bfloat16),
            pltpu.VMEM((1, devices), jnp.int32),
            pltpu.SMEM((1, devices), jnp.int32),
            pltpu.SMEM((1, devices), jnp.int32),
            pltpu.SMEM((1, devices), jnp.int32),
            pltpu.VMEM((1, devices), jnp.int32),
            pltpu.VMEM((1, devices), jnp.int32),
            pltpu.SemaphoreType.REGULAR,
            pltpu.SemaphoreType.DMA(()),
            pltpu.SemaphoreType.DMA(()),
            pltpu.SemaphoreType.DMA((reps,)),
            pltpu.SemaphoreType.DMA((4,)),
            pltpu.SemaphoreType.DMA((2,)),
            pltpu.SemaphoreType.DMA((2,)),
            pltpu.SemaphoreType.DMA(()),
        ]
        + 2
        * [
            pltpu.SemaphoreType.DMA(()),
            pltpu.SemaphoreType.DMA((GROUPS,)),
            pltpu.SemaphoreType.DMA((2,)),
            pltpu.SemaphoreType.DMA((2,)),
        ],
        compiler_params=pltpu.CompilerParams(
            collective_id=0, has_side_effects=True, vmem_limit_bytes=40 << 20
        ),
        name="shampoo_step",
    )(
        keep(gradient), keep(block_lists.reshape(1, devices)), keep(block_counts.reshape(1, devices)),
        keep(left_stats), keep(right_stats),
    )
    results = (direction, left_new, right_new)
    return pl.pallas_call(
        hand_over,
        out_shape=tuple(jax.ShapeDtypeStruct(x.shape, x.dtype) for x in results),
        in_specs=[pl.BlockSpec(memory_space=pltpu.VMEM)] * 3,
        out_specs=(anywhere,) * 3,
        scratch_shapes=[pltpu.SemaphoreType.DMA((3, PIECES))],
        compiler_params=pltpu.CompilerParams(vmem_limit_bytes=16 << 20),
        name="hand_over",
    )(*results)


def solution(mesh):
    placed = (P("rep", None, "fsdp", None), P("fsdp", None, None), P("fsdp", None, None), P(), P())
    return jax.shard_map(
        local,
        mesh=mesh,
        in_specs=placed,
        out_specs=(P(None, "fsdp", None), P("fsdp", None, None), P("fsdp", None, None)),
        check_vma=False,
    )
```

```python
import functools

import jax
import jax.numpy as jnp
from jax import lax
from jax.experimental import pallas as pl
from jax.experimental.pallas import tpu as pltpu
from jax.sharding import PartitionSpec as P

DECAY = 0.95
LANES = 8
MESH = pl.DeviceIdType.MESH
PIECES = 2
GROUPS = 4


def near_first(count):
    order = [0]
    for step in range(1, count // 2 + 1):
        order.append(step)
        if count - step != step:
            order.append(count - step)
    return order


def groups_of(layers, cuts):
    ends = [0] + [cut * layers // 16 for cut in cuts] + [layers]
    return [(lo, hi) for lo, hi in zip(ends, ends[1:]) if hi > lo]


def position():
    rep, place = lax.axis_index("rep"), lax.axis_index("fsdp")
    return rep, place, place // LANES, place % LANES


def reach_of(layers):
    return (layers // 2 + 1) // 2


def greet(reps, layers, relay):
    rep, place, layer, lane = position()
    reach = reach_of(layers)
    barrier = pltpu.get_barrier_semaphore()
    peers = []
    for step in range(reach, 0, -1):
        for way in (step, layers - step):
            peers.append((rep, ((layer + way) % layers) * LANES + lane))
    peers += [((rep + turn) % reps, place) for turn in range(1, reps)]
    peers += [(rep, layer * LANES + (lane + hop) % LANES) for hop in range(1, LANES)]
    for peer in peers:
        pl.semaphore_signal(barrier, inc=1, device_id=peer, device_id_type=MESH)
    pl.semaphore_wait(barrier, len(peers))
    for way in (reach, layers - reach):
        there = ((layer + way) % layers) * LANES + lane
        pl.semaphore_signal(relay, inc=1, device_id=(rep, there), device_id_type=MESH)


def take(ref, sem):
    pltpu.make_async_copy(ref, ref, sem).wait()


def exchange(reps, layers, cuts, order_a, send, mid, out, a_send, a_recv, b_send, b_recv):
    rep, _, layer, lane = position()
    order = near_first(layers)
    groups = groups_of(layers, cuts)
    for slot in order_a:
        there = (layer - order[slot] + layers) % layers
        group = [lo <= slot < hi for lo, hi in groups].index(True)
        pltpu.make_async_remote_copy(
            src_ref=send.at[there],
            dst_ref=mid.at[:, slot],
            send_sem=a_send,
            recv_sem=a_recv.at[group],
            device_id=(rep, there * LANES + lane),
            device_id_type=MESH,
        ).start()
    mid[:, 0] = send[layer]
    for group, (lo, hi) in enumerate(groups):
        if max(lo, 1) < hi:
            take(mid.at[:, max(lo, 1) : hi], a_recv.at[group])
        for turn in [t for t in (2, 1, 3) if t < reps] + [0]:
            for hop in (4, 6, 2, 5, 3, 7, 1, 0):
                if turn or hop:
                    target = (lane + hop) % LANES
                    pltpu.make_async_remote_copy(
                        src_ref=mid.at[target, lo:hi],
                        dst_ref=out.at[rep, lo:hi, lane],
                        send_sem=b_send.at[min(turn, 1)],
                        recv_sem=b_recv.at[min(turn, 1)],
                        device_id=((rep + turn) % reps, layer * LANES + target),
                        device_id_type=MESH,
                    ).start()
    out[rep, :, lane] = mid[lane]
    take(out.at[0 : reps - 1], b_recv.at[1])
    take(out.at[0, 0 : layers - layers // LANES], b_recv.at[0])


def exchange_end(reps, layers, mid, out, a_send, b_send):
    take(mid.at[:, 1:], a_send)
    take(out.at[0 : reps - 1], b_send.at[1])
    take(out.at[0, 0 : layers - layers // LANES], b_send.at[0])


def mm(a, b, dims=((1,), (0,))):
    return lax.dot_general(a, b, (dims, ((), ())), preferred_element_type=jnp.float32)


def root(stat):
    size = stat.shape[0]
    bound = jnp.max(jnp.sum(jnp.abs(stat), axis=0, keepdims=True))
    factor = 2.5 / bound
    row = lax.broadcasted_iota(jnp.int32, (size, size), 0)
    col = lax.broadcasted_iota(jnp.int32, (size, size), 1)
    diagonal = row == col
    d = jnp.where(diagonal, 0.25, 0.0) - (0.25 * factor) * stat
    low = d.astype(jnp.bfloat16)
    e = 2.0 * d + mm(low, low)
    low = e.astype(jnp.bfloat16)
    k = 2.0 * e + mm(low, low)
    j = 5.0 * d - 4.0 * e
    kj = mm(k.astype(jnp.bfloat16), j.astype(jnp.bfloat16))
    gain = jnp.sqrt(jnp.sqrt(factor))
    return (gain * (jnp.where(diagonal, 1.0, 0.0) + e - 0.25 * (k + kj))).astype(jnp.bfloat16)


def kernel(
    reps, layers, grad, ids_in, counts_in, left, right,
    arrived, table, left_out, right_out,
    local, parts, total, send, mid_in, blocks, g_ref, stat_left, stat_right, left_new, right_new, shaped,
    piece, mid_out, ids, counts, ids_row, counts_row,
    relay, r_send, r_recv, fetch_sems, small_sems, stat_sems, put_sems,
    a_send, a_recv, b_send, b_recv, c_send, c_recv, d_send, d_recv,
):
    rep, place, layer, lane = position()
    block_total, dev_rows, width = total.shape
    rows = LANES * dev_rows
    fetch = []
    for part in range(reps):
        fetch.append(
            pltpu.make_async_copy(
                grad.at[0, :, :, part * width : (part + 1) * width], local.at[part], fetch_sems.at[part]
            )
        )
        fetch[-1].start()
    greet(reps, layers, relay)
    for copy in fetch:
        copy.wait()

    for turn in [t for t in (2, 1, 3) if t < reps]:
        there = (rep + turn) % reps
        pltpu.make_async_remote_copy(
            src_ref=local.at[there],
            dst_ref=parts.at[turn],
            send_sem=r_send,
            recv_sem=r_recv,
            device_id=(there, place),
            device_id_type=MESH,
        ).start()

    small = [
        pltpu.make_async_copy(ids_in, ids, small_sems.at[0]),
        pltpu.make_async_copy(counts_in, counts, small_sems.at[1]),
        pltpu.make_async_copy(ids_in, ids_row, small_sems.at[2]),
        pltpu.make_async_copy(counts_in, counts_row, small_sems.at[3]),
    ]
    get_left = pltpu.make_async_copy(left.at[0], stat_left, stat_sems.at[0])
    get_right = pltpu.make_async_copy(right.at[0], stat_right, stat_sems.at[1])
    for copy in (*small, get_left, get_right):
        copy.start()
    for copy in small:
        copy.wait()

    devices = layers * LANES
    worker = lax.broadcasted_iota(jnp.int32, (devices, devices), 0)
    named = jnp.where(counts_row[...] > 0, ids_row[...], -1)
    named = jnp.transpose(jnp.broadcast_to(named, (devices, devices)))
    match = named == lax.broadcasted_iota(jnp.int32, (devices, devices), 1)
    offset = (worker // LANES - layer + layers) % layers
    slot = jnp.where(offset <= layers // 2, jnp.maximum(2 * offset - 1, 0), 2 * (layers - offset))
    spot = slot * LANES + worker % LANES
    table[...] = jnp.max(jnp.where(match, spot, 0), axis=0, keepdims=True)

    take(parts.at[1:reps], r_recv)
    acc = local[rep].astype(jnp.float32)
    for turn in range(1, reps):
        acc = acc + parts[turn].astype(jnp.float32)
    total[...] = acc.astype(jnp.bfloat16)

    @pl.loop(0, layers)
    def _(z):
        for l in range(LANES):
            block = jnp.clip(ids[0, z * LANES + l], 0, block_total - 1)
            send[z, l] = total[block]

    pl.semaphore_wait(relay, 2)
    far_first = range(layers - 1, 0, -1)
    exchange(reps, layers, (3,), far_first, send, mid_in, blocks, a_send, a_recv, b_send, b_recv)

    for part in range(reps):
        for slot_at, offset_at in enumerate(near_first(layers)):
            start = pl.multiple_of(((layer + offset_at) % layers) * rows, rows)
            g_ref[pl.ds(start, rows), part * width : (part + 1) * width] = blocks[
                part, slot_at
            ].reshape(rows, width)
    g = g_ref[...]
    used = counts[0, place] > 0
    get_left.wait()
    get_right.wait()
    old = stat_left[...]
    left_new[...] = jnp.where(used, DECAY * old + (1.0 - DECAY) * mm(g, g, ((1,), (1,))), old)
    left_out[0] = left_new[...]
    old = stat_right[...]
    right_new[...] = jnp.where(used, DECAY * old + (1.0 - DECAY) * mm(g, g, ((0,), (0,))), old)
    right_out[0] = right_new[...]
    left_root = root(left_new[...])
    right_root = root(right_new[...])
    half = mm(left_root, g).astype(jnp.bfloat16)
    shaped[...] = mm(half, right_root)
    wide = g.astype(jnp.float32)
    grad_norm = jnp.sqrt(jnp.sum(wide * wide))
    whole = shaped[...]
    shaped_norm = jnp.sqrt(jnp.sum(whole * whole) + 1e-06)
    own = shaped[:, pl.ds(pl.multiple_of(rep * width, width), width)]
    grafted = (own * (grad_norm / shaped_norm)).astype(jnp.bfloat16)
    piece[...] = grafted.reshape(piece.shape)

    exchange(reps, layers, (5, 11), range(1, layers), piece, mid_out, arrived, c_send, c_recv, d_send, d_recv)
    take(parts.at[1:reps], r_send)
    exchange_end(reps, layers, mid_in, blocks, a_send, b_send)
    exchange_end(reps, layers, mid_out, arrived, c_send, d_send)


def hand_over(
    arrived, table, left, right, direction_out, left_out, right_out, direction, spots, sems, own_sems
):
    reps, _, _, _, width = arrived.shape
    get_table = pltpu.make_async_copy(table, spots, own_sems.at[0])
    get_table.start()
    copies = []
    for k, (src, dst) in enumerate([(left.at[0], left_out.at[0]), (right.at[0], right_out.at[0])]):
        step = src.shape[0] // PIECES
        for p in range(PIECES):
            span = pl.ds(p * step, step)
            copies.append(pltpu.make_async_copy(src.at[span], dst.at[span], sems.at[k, p]))
    for copy in copies:
        copy.start()
    get_table.wait()

    @pl.loop(0, direction.shape[0] // 8)
    def _(group):
        for k in range(8):
            block = group * 8 + k
            spot = spots[0, block]
            for part in range(reps):
                direction[block, :, part * width : (part + 1) * width] = arrived[
                    part, spot // LANES, spot % LANES
                ]

    put = pltpu.make_async_copy(direction, direction_out, own_sems.at[1])
    put.start()
    for copy in copies:
        copy.wait()
    put.wait()


def local(gradient, left_stats, right_stats, block_lists, block_counts):
    _, block_total, dev_rows, cols = gradient.shape
    reps, devices = lax.axis_size("rep"), lax.axis_size("fsdp")
    layers = devices // LANES
    width = cols // reps
    rows = devices * dev_rows
    vmem = pl.BlockSpec(memory_space=pltpu.VMEM)
    anywhere = pl.BlockSpec(memory_space=pl.ANY)
    def keep(x):
        return pltpu.with_memory_space_constraint(x, pltpu.HBM)

    arrived, table, left_new, right_new = pl.pallas_call(
        functools.partial(kernel, reps, layers),
        out_shape=(
            pltpu.VMEM((reps, layers, LANES, dev_rows, width), jnp.bfloat16),
            pltpu.VMEM((1, devices), jnp.int32),
            pltpu.VMEM(left_stats.shape, jnp.float32),
            pltpu.VMEM(right_stats.shape, jnp.float32),
        ),
        in_specs=[anywhere] * 5,
        out_specs=(vmem, vmem, vmem, vmem),
        scratch_shapes=[
            pltpu.VMEM((reps, block_total, dev_rows, width), jnp.bfloat16),
            pltpu.VMEM((reps, block_total, dev_rows, width), jnp.bfloat16),
            pltpu.VMEM((block_total, dev_rows, width), jnp.bfloat16),
            pltpu.VMEM((layers, LANES, dev_rows, width), jnp.bfloat16),
            pltpu.VMEM((LANES, layers, dev_rows, width), jnp.bfloat16),
            pltpu.VMEM((reps, layers, LANES, dev_rows, width), jnp.bfloat16),
            pltpu.VMEM((rows, cols), jnp.bfloat16),
            pltpu.VMEM((rows, rows), jnp.float32),
            pltpu.VMEM((cols, cols), jnp.float32),
            pltpu.VMEM((rows, rows), jnp.float32),
            pltpu.VMEM((cols, cols), jnp.float32),
            pltpu.VMEM((rows, cols), jnp.float32),
            pltpu.VMEM((layers, LANES, dev_rows, width), jnp.bfloat16),
            pltpu.VMEM((LANES, layers, dev_rows, width), jnp.bfloat16),
            pltpu.SMEM((1, devices), jnp.int32),
            pltpu.SMEM((1, devices), jnp.int32),
            pltpu.VMEM((1, devices), jnp.int32),
            pltpu.VMEM((1, devices), jnp.int32),
            pltpu.SemaphoreType.REGULAR,
            pltpu.SemaphoreType.DMA(()),
            pltpu.SemaphoreType.DMA(()),
            pltpu.SemaphoreType.DMA((reps,)),
            pltpu.SemaphoreType.DMA((4,)),
            pltpu.SemaphoreType.DMA((2,)),
            pltpu.SemaphoreType.DMA((2,)),
        ]
        + 2
        * [
            pltpu.SemaphoreType.DMA(()),
            pltpu.SemaphoreType.DMA((GROUPS,)),
            pltpu.SemaphoreType.DMA((2,)),
            pltpu.SemaphoreType.DMA((2,)),
        ],
        compiler_params=pltpu.CompilerParams(
            collective_id=0, has_side_effects=True, vmem_limit_bytes=40 << 20
        ),
        name="shampoo_step",
    )(
        keep(gradient), keep(block_lists.reshape(1, devices)), keep(block_counts.reshape(1, devices)),
        keep(left_stats), keep(right_stats),
    )
    results = (
        jax.ShapeDtypeStruct((block_total, dev_rows, cols), jnp.bfloat16), left_new, right_new
    )
    return pl.pallas_call(
        hand_over,
        out_shape=tuple(jax.ShapeDtypeStruct(x.shape, x.dtype) for x in results),
        in_specs=[vmem] * 4,
        out_specs=(anywhere,) * 3,
        scratch_shapes=[
            pltpu.VMEM((block_total, dev_rows, cols), jnp.bfloat16),
            pltpu.SMEM((1, devices), jnp.int32),
            pltpu.SemaphoreType.DMA((2, PIECES)),
            pltpu.SemaphoreType.DMA((2,)),
        ],
        compiler_params=pltpu.CompilerParams(vmem_limit_bytes=16 << 20),
        name="hand_over",
    )(arrived, table, left_new, right_new)


def solution(mesh):
    placed = (P("rep", None, "fsdp", None), P("fsdp", None, None), P("fsdp", None, None), P(), P())
    return jax.shard_map(
        local,
        mesh=mesh,
        in_specs=placed,
        out_specs=(P(None, "fsdp", None), P("fsdp", None, None), P("fsdp", None, None)),
        check_vma=False,
    )
```
